256 devices in a mesh: dp: 2 (over x_lo), row: 16 (over z, core), col: 8 (over x_hi, y).
Axes of the slice: x: 4 (x_hi: 2, x_lo: 2; x = x_hi * 2 + x_lo), y: 4, z: 8, core: 2. Of those that a mesh axis runs over, the one named last changes fastest.
Arguments:
- grad_parts: bfloat16 [2, 2, 2048, 8, 2048], P('dp', None, 'row', None, 'col'), may hold values from -6 to 6
- out_basis: bfloat16 [2, 2048, 2048], P('dp', None, 'row'), may hold values from -0.125 to 0.125
- in_basis: bfloat16 [8, 2048, 2048], P('col'), may hold values from -0.125 to 0.125
- moments: float32 [2, 2048, 8, 2048], P('dp', 'row', 'col'), may hold values from 0.05 to 1
Outputs:
- moments_next: float32 [2, 2048, 8, 2048], P('dp', 'row', 'col')
- update: bfloat16 [2, 2048, 8, 2048], P('dp', 'row', 'col')
The draws below stay inside these ranges and needn't reach their ends.
All inputs are finite; a program needn't handle non-finite values.
Results may differ from the reference program's by a relative error of at most 0.027.
Values may be sent and summed in bfloat16 or wider, within the bound.
No kernel may reach another device: no remote copies, remote signals or barrier semaphores. Data moves between devices by JAX's collectives and lax.ppermute only.
A program may use at most 64 MiB of HBM per device.

```python
import math
import jax
import jax.numpy as jnp

BO = 2048
BI = 2048
NBO = 2
NBI = 8
N_DP = 2


def raised(values, own_key, source, target, shards_of, factor):
    def block_of(position):
        return (jnp.arange(values.shape[position]) // (values.shape[position] // shards_of)).reshape((-1,) + (1,) * (values.ndim - 1 - position))

    one_side = jax.random.permutation(own_key, shards_of)[block_of(target)]
    second = (block_of(target) + shards_of // 2) % shards_of
    return jnp.where((block_of(source) == one_side) | (block_of(source) == second), factor * values, values)


def level_of(key, extent, cuts, least, top_value):
    def one(position, blocks):
        steps = jax.random.uniform(jax.random.fold_in(jax.random.fold_in(key, 6), position), (blocks,), jnp.float32, least / len(cuts), top_value / len(cuts))
        return jnp.repeat(jnp.exp(steps), extent[position] // blocks).reshape((-1,) + (1,) * (len(extent) - position - 1))

    loudness = one(*cuts[0])
    for cut in cuts[1:]:
        loudness = loudness * one(*cut)
    return loudness


def normal_values(stream_key, shape, spread, most, split=(), dtype=jnp.bfloat16):
    result = spread * jax.random.normal(stream_key, shape, jnp.float32)
    if split:
        result = result * level_of(stream_key, shape, split, -0.22, 0.18)
    return jnp.clip(result, -most, most).astype(dtype)


def bell_draw_with(key, shape, spread, limit, split, heavy, kind=jnp.bfloat16):
    array = spread * jax.random.normal(key, shape, jnp.float32)
    if split:
        array = array * level_of(key, shape, split, -0.22, 0.18)
    return jnp.clip(raised(array, jax.random.fold_in(key, 3), *heavy), -limit, limit).astype(kind)


def setup_inputs(seed: int = 0) -> dict:
    streams_of = jax.random.split(jax.random.key(seed), 5)
    return {
        "grad_parts": bell_draw_with(streams_of[0], (N_DP, NBO, BO, NBI, BI), 1.0, 6.0, ((0, 2), (2, 16), (4, 8)), (0, 1, 2, 2.0)),
        "out_basis": normal_values(streams_of[1], (NBO, BO, BO), BO ** -0.5, 0.125, ((0, 2), (2, 16))),
        "in_basis": normal_values(streams_of[2], (NBI, BI, BI), BI ** -0.5, 0.125, ((0, 8),)),
        "moments": jnp.clip(jnp.exp(math.log(1.0) - 2.9957323 * jax.random.uniform(streams_of[3], (NBO, BO, NBI, BI), jnp.float32) ** level_of(streams_of[3], (NBO, BO, NBI, BI), ((0, 2), (1, 16), (2, 8)), -0.2, 0.2)), 0.05, 1.0),
    }


ema_decay = 0.9
damping = 0.1


def reference(grad_parts, out_basis, in_basis, moments):
    gradient = jnp.sum(grad_parts.astype(jnp.float32), axis=0).astype(jnp.bfloat16)
    in_float = in_basis.astype(jnp.float32)
    out_float = out_basis.astype(jnp.float32)
    half_rotated = jnp.einsum('bkjc,jcd->bkjd', gradient.astype(jnp.float32), in_float).astype(jnp.bfloat16)
    rotated = jnp.einsum('bkr,bkjd->brjd', out_float, half_rotated.astype(jnp.float32))
    moments_next = ema_decay * moments + (1.0 - ema_decay) * rotated * rotated
    scaled = (rotated / (moments_next + damping)).astype(jnp.bfloat16)
    turned_back = jnp.einsum('bkr,brjd->bkjd', out_float, scaled.astype(jnp.float32)).astype(jnp.bfloat16)
    update = jnp.einsum('bkjd,jcd->bkjc', turned_back.astype(jnp.float32), in_float).astype(jnp.bfloat16)
    return moments_next, update
```

```python
import jax
import jax.numpy as jnp
from jax import lax
from jax.sharding import PartitionSpec as P

ema_decay = 0.9
damping = 0.1


def shards(grad_parts, out_basis, in_basis, moments):
    f32, bf16 = jnp.float32, jnp.bfloat16
    rows, blocks, width = grad_parts.shape[2:]
    count = out_basis.shape[1] // rows
    order = in_basis.shape[1]
    chunk = order // count

    basis = lax.all_gather(out_basis[0], "row", axis=0, tiled=False)
    sent = grad_parts[0].transpose(0, 2, 1, 3).reshape(-1, rows, width)
    parts = lax.all_to_all(sent, ("dp", "col"), split_axis=0, concat_axis=0, tiled=True)
    parts = parts.reshape(-1, blocks, rows, width)
    gradient = jnp.sum(parts.astype(f32), axis=0).astype(bf16)
    half = lax.dot_general(
        gradient.transpose(1, 0, 2).reshape(rows, order),
        in_basis[0],
        (((1,), (0,)), ((), ())),
        preferred_element_type=f32,
    ).astype(bf16)
    moment_rows = moments.reshape(rows, order)

    def to_columns(x):
        return x.reshape(rows, count, chunk).transpose(1, 0, 2)

    both = jnp.stack([to_columns(half), to_columns(moment_rows.astype(bf16))], axis=1)
    both = lax.all_to_all(both, "row", split_axis=0, concat_axis=0, tiled=True)
    half_cols = both[:, 0].reshape(-1, chunk)
    moment_cols = both[:, 1].astype(f32)
    rotated = jnp.einsum("pkr,kd->prd", basis, half_cols, preferred_element_type=f32)
    scaled = (
        rotated
        / (ema_decay * moment_cols + (1.0 - ema_decay) * rotated * rotated + damping)
    ).astype(bf16)
    turned = jnp.einsum("pkr,prd->kd", basis, scaled, preferred_element_type=f32)
    turned = turned.astype(bf16).reshape(count, rows, chunk)
    back = jnp.stack([turned, rotated.astype(bf16)], axis=1)
    back = lax.all_to_all(back, "row", split_axis=0, concat_axis=0, tiled=True)
    turned_rows = back[:, 0].transpose(1, 0, 2).reshape(rows, order)
    rotated_rows = back[:, 1].astype(f32).transpose(1, 0, 2).reshape(rows, order)
    update = lax.dot_general(
        turned_rows,
        in_basis[0],
        (((1,), (1,)), ((), ())),
        preferred_element_type=f32,
    ).astype(bf16)
    new_moments = ema_decay * moment_rows + (1.0 - ema_decay) * rotated_rows * rotated_rows
    return (
        new_moments.reshape(1, rows, 1, order),
        update.reshape(1, rows, 1, order),
    )


def solution(mesh):
    placed = (
        P("dp", None, "row", None, "col"),
        P("dp", None, "row"),
        P("col", None, None),
        P("dp", "row", "col", None),
    )
    return jax.shard_map(
        shards,
        mesh=mesh,
        in_specs=placed,
        out_specs=(P("dp", "row", "col", None), P("dp", "row", "col", None)),
        check_vma=False,
    )
```

```python
import jax
import jax.numpy as jnp
from jax import lax
from jax.experimental import pallas as pl
from jax.experimental.pallas import tpu as pltpu
from jax.sharding import PartitionSpec as P

ema_decay = 0.9
damping = 0.1
f32, bf16 = jnp.float32, jnp.bfloat16
VMEM = pl.BlockSpec(memory_space=pltpu.VMEM)
SMEM = pl.BlockSpec(memory_space=pltpu.SMEM)
ANY = pl.BlockSpec(memory_space=pl.ANY)


def limit(mib):
    return pltpu.CompilerParams(vmem_limit_bytes=mib * 1024 * 1024)


def half_kernel(parts, basis, moment, out, pair, held, flat, total, arrive):
    blocks, rows, width = parts.shape[1:]
    wide = out.shape[3]
    copies = []
    for j in range(blocks):
        at = pl.ds(j * width, width)
        copies.append(pltpu.make_async_copy(parts.at[:, j], pair.at[:, j], arrive.at[0, j]))
        copies.append(pltpu.make_async_copy(basis.at[at], held.at[at], arrive.at[1, j]))
    copies.append(pltpu.make_async_copy(moment, flat, arrive.at[2, 0]))
    for copy in copies:
        copy.start()
    for j in range(blocks):
        copies[2 * j].wait()
        grad = (pair[0, j].astype(f32) + pair[1, j].astype(f32)).astype(bf16)
        copies[2 * j + 1].wait()
        part = jnp.dot(grad, held[j * width : (j + 1) * width], preferred_element_type=f32)
        if j == 0:
            total[...] = part
        elif j < blocks - 1:
            total[...] += part
        else:
            part = (total[...] + part).astype(bf16)
    copies[-1].wait()
    for i in range(out.shape[0]):
        out[i, 0] = part[:, i * wide : (i + 1) * wide]
        out[i, 1] = flat[:, i * wide : (i + 1) * wide].astype(bf16)


def half_rotate(parts, basis, moments, count):
    rows, order = moments.shape
    return pl.pallas_call(
        half_kernel,
        in_specs=[ANY] * 3,
        out_specs=VMEM,
        out_shape=jax.ShapeDtypeStruct((count, 2, rows, order // count), bf16),
        scratch_shapes=[
            pltpu.VMEM(parts.shape, bf16),
            pltpu.VMEM(basis.shape, bf16),
            pltpu.VMEM(moments.shape, f32),
            pltpu.VMEM(moments.shape, f32),
            pltpu.SemaphoreType.DMA((3, parts.shape[1])),
        ],
        compiler_params=limit(50),
        cost_estimate=pl.CostEstimate(
            flops=2 * rows * order * order, bytes_accessed=2 * order * order, transcendentals=0
        ),
        name="half_rotate",
    )(parts, basis, moments)


def stack_kernel(*refs):
    out = refs[-1]
    for i, ref in enumerate(refs[:-1]):
        out[i] = ref[...]


def stack(pieces):
    return pl.pallas_call(
        stack_kernel,
        in_specs=[VMEM] * len(pieces),
        out_specs=VMEM,
        out_shape=jax.ShapeDtypeStruct((len(pieces),) + pieces[0].shape, pieces[0].dtype),
        compiler_params=limit(8),
        cost_estimate=pl.CostEstimate(flops=0, bytes_accessed=1 << 25, transcendentals=0),
        name="stack",
    )(*pieces)


offsets = (0, -1, 1, -2, 2, -3, 3, 4)


def rotate_kernel(place, mine, *refs):
    sources, (out, flipped, scaled, held, arrive) = refs[:8], refs[8:]
    chip, core, first = place[0], place[1], place[2]
    starts = [lax.rem(first + i, 4) for i in (0, 3, 1, 2)]
    count, _, rows, width = out.shape
    chips, per = count // 2, count // 4
    copies = [
        [
            pltpu.make_async_copy(
                sources[i].at[pl.ds(2 * n, 2)], held.at[i, pl.ds(2 * n, 2)], arrive.at[n, i]
            )
            for i in range(8)
        ]
        for n in range(4)
    ]
    for some in copies:
        for copy in some:
            copy.start()
    for q in range(4):
        flipped[q] = mine[q * per : (q + 1) * per, 0].reshape(per * rows, width).T
    for n in range(8):
        if n % 2 == 0:
            for copy in copies[n // 2]:
                copy.wait()
        both = jnp.zeros((width, 2 * rows), f32)
        for q in range(4):
            rhs = jnp.concatenate(
                [held[4 * p + q, n].reshape(per * rows, rows) for p in range(2)], axis=1
            )
            both += jnp.dot(flipped[starts[q]], rhs, preferred_element_type=f32)
        for p in range(2):
            value = both[:, p * rows : (p + 1) * rows].T
            at = 2 * lax.rem(chip + offsets[n] + chips, chips) + (core if p == 0 else 1 - core)
            moment = mine[at, 1].astype(f32)
            out[at, 1] = value.astype(bf16)
            moment = ema_decay * moment + (1.0 - ema_decay) * value * value
            at = (2 * n + p) * rows
            scaled[at : at + rows] = (value / (moment + damping)).astype(bf16)
    for q in range(4):
        lhs = jnp.concatenate(
            [held[4 * p + q, n].reshape(per * rows, rows) for n in range(8) for p in range(2)],
            axis=1,
        )
        part = jnp.dot(lhs, scaled[...], preferred_element_type=f32)
        out[pl.ds(starts[q] * per, per), 0] = part.reshape(per, rows, width).astype(bf16)


def rotate(place, mine, sources):
    count, _, rows, width = mine.shape
    return pl.pallas_call(
        rotate_kernel,
        in_specs=[SMEM, VMEM] + [ANY] * 8,
        out_specs=VMEM,
        out_shape=jax.ShapeDtypeStruct(mine.shape, bf16),
        scratch_shapes=[
            pltpu.VMEM((4, width, count // 4 * rows), bf16),
            pltpu.VMEM((count * rows, width), bf16),
            pltpu.VMEM((8,) + sources[0].shape, bf16),
            pltpu.SemaphoreType.DMA((4, 8)),
        ],
        compiler_params=limit(24),
        cost_estimate=pl.CostEstimate(flops=1 << 32, bytes_accessed=1 << 25, transcendentals=0),
        name="rotate",
    )(place, mine, *sources)


def update_kernel(back, basis, moment, update, moment_next, turned):
    count, _, _, width = back.shape
    for i in range(count):
        at = slice(i * width, (i + 1) * width)
        turned[:, at] = back[i, 0]
        rotated = back[i, 1].astype(f32)
        moment_next[:, at] = ema_decay * moment[:, at] + (1.0 - ema_decay) * rotated * rotated
    step = 256
    for i in range(0, basis.shape[0], step):
        update[:, i : i + step] = lax.dot_general(
            turned[...], basis[i : i + step], (((1,), (1,)), ((), ())), preferred_element_type=f32
        ).astype(bf16)


def finish(back, basis, moments):
    rows, order = moments.shape
    return pl.pallas_call(
        update_kernel,
        in_specs=[VMEM] * 3,
        out_specs=[VMEM] * 2,
        out_shape=[
            jax.ShapeDtypeStruct((rows, order), bf16),
            jax.ShapeDtypeStruct((rows, order), f32),
        ],
        scratch_shapes=[pltpu.VMEM((rows, order), bf16)],
        compiler_params=limit(16),
        name="finish",
    )(back, basis, moments)


def shards(grad_parts, out_basis, in_basis, moments):
    rows, blocks, width = grad_parts.shape[2:]
    order = in_basis.shape[1]
    row, col = lax.axis_index("row"), lax.axis_index("col")
    count = lax.axis_size("row")
    chips = count // 2
    up = [(i, (i + 2) % count) for i in range(count)]
    down = [(b, a) for a, b in up]
    swap = [(i, i ^ 1) for i in range(count)]
    y_next = [(4 * h + y, 4 * h + (y + 1) % 4) for h in range(2) for y in range(4)]
    y_last = [(b, a) for a, b in y_next]
    x_swap = [(i, (i + 4) % 8) for i in range(8)]
    quarter = (col + 2 * (col >> 2)) & 3
    place = jnp.stack([row >> 1, row & 1, quarter]).astype(jnp.int32)

    own = lax.dynamic_slice_in_dim(out_basis[0], quarter * (order // 4), order // 4, 0)
    own = own.reshape(chips // 4, 2, rows, rows)
    a, b = lax.ppermute(own, "row", up), lax.ppermute(own, "row", down)

    sent = grad_parts[0].transpose(0, 2, 1, 3).reshape(-1, rows, width)
    parts = lax.all_to_all(sent, ("dp", "col"), split_axis=0, concat_axis=0, tiled=True)
    parts = parts.reshape(2, blocks, rows, width)

    near = [own, a, b]
    flat = moments.reshape(rows, order)
    a, b, flat = lax.optimization_barrier((a, b, flat))
    for _ in range(2):
        a, b = lax.ppermute(a, "row", up), lax.ppermute(b, "row", down)
        near += [a, b]
    near.append(lax.ppermute(a, "row", up))
    half = half_rotate(parts, in_basis[0], flat, count)
    half, near = lax.optimization_barrier((half, near))
    held = stack(near)
    quarters = [held]
    for pairs in (y_next, y_last, x_swap):
        quarters.append(lax.ppermute(held, "col", pairs))
    quarters += [lax.ppermute(x, "row", swap) for x in quarters]
    half = lax.all_to_all(half, "row", split_axis=0, concat_axis=0, tiled=True)
    back = rotate(place, half, quarters)
    back = lax.all_to_all(back, "row", split_axis=0, concat_axis=0, tiled=True)
    update, new_moments = finish(back, in_basis[0], flat)
    return new_moments.reshape(1, rows, 1, order), update.reshape(1, rows, 1, order)


def solution(mesh):
    placed = (
        P("dp", None, "row", None, "col"),
        P("dp", None, "row"),
        P("col", None, None),
        P("dp", "row", "col", None),
    )
    return jax.shard_map(
        shards,
        mesh=mesh,
        in_specs=placed,
        out_specs=(P("dp", "row", "col", None), P("dp", "row", "col", None)),
        check_vma=False,
    )
```

```python
import jax
import jax.numpy as jnp
from jax import lax
from jax.experimental import pallas as pl
from jax.experimental.pallas import tpu as pltpu
from jax.sharding import PartitionSpec as P

ema_decay = 0.9
damping = 0.1
f32, bf16 = jnp.float32, jnp.bfloat16
VMEM = pl.BlockSpec(memory_space=pltpu.VMEM)
SMEM = pl.BlockSpec(memory_space=pltpu.SMEM)
ANY = pl.BlockSpec(memory_space=pl.ANY)


def limit(mib):
    return pltpu.CompilerParams(vmem_limit_bytes=mib * 1024 * 1024)


def half_kernel(parts, basis, moment, out, pair, held, flat, total, arrive):
    blocks, rows, width = parts.shape[1:]
    wide = out.shape[3]
    copies = []
    for j in range(blocks):
        at = pl.ds(j * width, width)
        copies.append(pltpu.make_async_copy(parts.at[:, j], pair.at[:, j], arrive.at[0, j]))
        copies.append(pltpu.make_async_copy(basis.at[at], held.at[at], arrive.at[1, j]))
    copies.append(pltpu.make_async_copy(moment, flat, arrive.at[2, 0]))
    for copy in copies:
        copy.start()
    for j in range(blocks):
        copies[2 * j].wait()
        grad = (pair[0, j].astype(f32) + pair[1, j].astype(f32)).astype(bf16)
        copies[2 * j + 1].wait()
        part = jnp.dot(grad, held[j * width : (j + 1) * width], preferred_element_type=f32)
        if j == 0:
            total[...] = part
        elif j < blocks - 1:
            total[...] += part
        else:
            part = (total[...] + part).astype(bf16)
    copies[-1].wait()
    for i in range(out.shape[0]):
        out[i, 0] = part[:, i * wide : (i + 1) * wide]
        out[i, 1] = flat[:, i * wide : (i + 1) * wide].astype(bf16)


def half_rotate(parts, basis, moments, count):
    rows, order = moments.shape
    return pl.pallas_call(
        half_kernel,
        in_specs=[ANY] * 3,
        out_specs=VMEM,
        out_shape=jax.ShapeDtypeStruct((count, 2, rows, order // count), bf16),
        scratch_shapes=[
            pltpu.VMEM(parts.shape, bf16),
            pltpu.VMEM(basis.shape, bf16),
            pltpu.VMEM(moments.shape, f32),
            pltpu.VMEM(moments.shape, f32),
            pltpu.SemaphoreType.DMA((3, parts.shape[1])),
        ],
        compiler_params=limit(50),
        cost_estimate=pl.CostEstimate(
            flops=2 * rows * order * order, bytes_accessed=2 * order * order, transcendentals=0
        ),
        name="half_rotate",
    )(parts, basis, moments)


def stack_kernel(*refs):
    out = refs[-1]
    for i, ref in enumerate(refs[:-1]):
        out[i] = ref[...]


def stack(pieces):
    return pl.pallas_call(
        stack_kernel,
        in_specs=[VMEM] * len(pieces),
        out_specs=VMEM,
        out_shape=jax.ShapeDtypeStruct((len(pieces),) + pieces[0].shape, pieces[0].dtype),
        compiler_params=limit(8),
        cost_estimate=pl.CostEstimate(flops=0, bytes_accessed=1 << 25, transcendentals=0),
        name="stack",
    )(*pieces)


offsets = (0, -1, 1, -2, 2, -3, 3, 4)


def rotate_kernel(place, mine, *refs):
    sources, (out, flipped, scaled, held, arrive) = refs[:8], refs[8:]
    chip, core, first = place[0], place[1], place[2]
    starts = [lax.rem(first + i, 4) for i in (0, 3, 1, 2)]
    count, _, rows, width = out.shape
    chips, per = count // 2, count // 4
    copies = [
        [
            pltpu.make_async_copy(
                sources[i].at[pl.ds(2 * n, 2)], held.at[i, pl.ds(2 * n, 2)], arrive.at[n, i]
            )
            for i in range(8)
        ]
        for n in range(4)
    ]
    for some in copies:
        for copy in some:
            copy.start()
    for q in range(4):
        flipped[q] = mine[q * per : (q + 1) * per, 0].reshape(per * rows, width).T
    for n in range(8):
        if n % 2 == 0:
            for copy in copies[n // 2]:
                copy.wait()
        both = jnp.zeros((width, 2 * rows), f32)
        for q in range(4):
            rhs = jnp.concatenate(
                [held[4 * p + q, n].reshape(per * rows, rows) for p in range(2)], axis=1
            )
            both += jnp.dot(flipped[starts[q]], rhs, preferred_element_type=f32)
        for p in range(2):
            value = both[:, p * rows : (p + 1) * rows].T
            at = 2 * lax.rem(chip + offsets[n] + chips, chips) + (core if p == 0 else 1 - core)
            moment = mine[at, 1].astype(f32)
            out[at, 1] = value.astype(bf16)
            moment = ema_decay * moment + (1.0 - ema_decay) * value * value
            at = (2 * n + p) * rows
            scaled[at : at + rows] = (value / (moment + damping)).astype(bf16)
    for q in range(4):
        lhs = jnp.concatenate(
            [held[4 * p + q, n].reshape(per * rows, rows) for n in range(8) for p in range(2)],
            axis=1,
        )
        part = jnp.dot(lhs, scaled[...], preferred_element_type=f32)
        out[pl.ds(starts[q] * per, per), 0] = part.reshape(per, rows, width).astype(bf16)


def rotate(place, mine, sources):
    count, _, rows, width = mine.shape
    return pl.pallas_call(
        rotate_kernel,
        in_specs=[SMEM, VMEM] + [ANY] * 8,
        out_specs=VMEM,
        out_shape=jax.ShapeDtypeStruct(mine.shape, bf16),
        scratch_shapes=[
            pltpu.VMEM((4, width, count // 4 * rows), bf16),
            pltpu.VMEM((count * rows, width), bf16),
            pltpu.VMEM((8,) + sources[0].shape, bf16),
            pltpu.SemaphoreType.DMA((4, 8)),
        ],
        compiler_params=limit(24),
        cost_estimate=pl.CostEstimate(flops=1 << 32, bytes_accessed=1 << 25, transcendentals=0),
        name="rotate",
    )(place, mine, *sources)


def flip_kernel(source, out):
    step = 256
    for i in range(0, source.shape[0], step):
        for j in range(0, source.shape[1], step):
            out[j : j + step, i : i + step] = source[i : i + step, j : j + step].T


def flip(basis):
    return pl.pallas_call(
        flip_kernel,
        in_specs=[VMEM],
        out_specs=VMEM,
        out_shape=jax.ShapeDtypeStruct(basis.shape, basis.dtype),
        compiler_params=limit(8),
        cost_estimate=pl.CostEstimate(flops=0, bytes_accessed=4 * basis.size, transcendentals=0),
        name="flip",
    )(basis)


def update_kernel(back, basis, moment, update, moment_next, turned, fresh, leave):
    count, _, _, width = back.shape
    for i in range(count):
        at = slice(i * width, (i + 1) * width)
        turned[:, at] = back[i, 0]
        rotated = back[i, 1].astype(f32)
        fresh[i] = ema_decay * moment[:, at] + (1.0 - ema_decay) * rotated * rotated
        pltpu.make_async_copy(fresh.at[i], moment_next.at[:, i, 0], leave.at[i]).start()
    step = 256
    for i in range(0, basis.shape[1], step):
        update[:, i : i + step] = jnp.dot(
            turned[...], basis[:, i : i + step], preferred_element_type=f32
        ).astype(bf16)
    for i in range(count):
        pltpu.make_async_copy(fresh.at[i], moment_next.at[:, i, 0], leave.at[i]).wait()


def finish(back, basis, moments):
    rows, order = moments.shape
    count = back.shape[0]
    return pl.pallas_call(
        update_kernel,
        in_specs=[VMEM] * 3,
        out_specs=[VMEM, ANY],
        out_shape=[
            jax.ShapeDtypeStruct((rows, order), bf16),
            jax.ShapeDtypeStruct((rows, count, 1, order // count), f32),
        ],
        scratch_shapes=[
            pltpu.VMEM((rows, order), bf16),
            pltpu.VMEM((count, rows, order // count), f32),
            pltpu.SemaphoreType.DMA((count,)),
        ],
        compiler_params=limit(16),
        name="finish",
    )(back, basis, moments)


def shards(grad_parts, out_basis, in_basis, moments):
    rows, blocks, width = grad_parts.shape[2:]
    order = in_basis.shape[1]
    row, col = lax.axis_index("row"), lax.axis_index("col")
    count = lax.axis_size("row")
    chips = count // 2
    up = [(i, (i + 2) % count) for i in range(count)]
    down = [(b, a) for a, b in up]
    swap = [(i, i ^ 1) for i in range(count)]
    y_next = [(4 * h + y, 4 * h + (y + 1) % 4) for h in range(2) for y in range(4)]
    y_last = [(b, a) for a, b in y_next]
    x_swap = [(i, (i + 4) % 8) for i in range(8)]
    quarter = (col + 2 * (col >> 2)) & 3
    place = jnp.stack([row >> 1, row & 1, quarter]).astype(jnp.int32)

    own = lax.dynamic_slice_in_dim(out_basis[0], quarter * (order // 4), order // 4, 0)
    own = own.reshape(chips // 4, 2, rows, rows)
    a, b = lax.ppermute(own, "row", up), lax.ppermute(own, "row", down)

    sent = grad_parts[0].transpose(0, 2, 1, 3).reshape(-1, rows, width)
    parts = lax.all_to_all(sent, ("dp", "col"), split_axis=0, concat_axis=0, tiled=True)
    parts = parts.reshape(2, blocks, rows, width)

    near = [own, a, b]
    flat = moments.reshape(rows, order)
    a, b, flat = lax.optimization_barrier((a, b, flat))
    for _ in range(2):
        a, b = lax.ppermute(a, "row", up), lax.ppermute(b, "row", down)
        near += [a, b]
    near.append(lax.ppermute(a, "row", up))
    half = half_rotate(parts, in_basis[0], flat, count)
    first, near = lax.optimization_barrier((half, near))
    held = stack(near)
    quarters = [held]
    for pairs in (y_next, y_last, x_swap):
        quarters.append(lax.ppermute(held, "col", pairs))
    quarters += [lax.ppermute(x, "row", swap) for x in quarters]
    half = lax.all_to_all(half, "row", split_axis=0, concat_axis=0, tiled=True)
    half, flipped = lax.optimization_barrier((half, flip(lax.optimization_barrier((in_basis[0], held))[0])))
    back = rotate(place, half, quarters)
    back = lax.all_to_all(back, "row", split_axis=0, concat_axis=0, tiled=True)
    update, new_moments = finish(back, flipped, flat)
    return new_moments.reshape(1, rows, 1, order), update.reshape(1, rows, 1, order)


def solution(mesh):
    placed = (
        P("dp", None, "row", None, "col"),
        P("dp", None, "row"),
        P("col", None, None),
        P("dp", "row", "col", None),
    )
    return jax.shard_map(
        shards,
        mesh=mesh,
        in_specs=placed,
        out_specs=(P("dp", "row", "col", None), P("dp", "row", "col", None)),
        check_vma=False,
    )
```

```python
import jax
import jax.numpy as jnp
from jax import lax
from jax.experimental import pallas as pl
from jax.experimental.pallas import tpu as pltpu
from jax.sharding import PartitionSpec as P

ema_decay = 0.9
damping = 0.1
f32, bf16 = jnp.float32, jnp.bfloat16
VMEM = pl.BlockSpec(memory_space=pltpu.VMEM)
SMEM = pl.BlockSpec(memory_space=pltpu.SMEM)
ANY = pl.BlockSpec(memory_space=pl.ANY)


def limit(mib):
    return pltpu.CompilerParams(vmem_limit_bytes=mib * 1024 * 1024)


def half_kernel(parts, basis, moment, out, pair, held, flat, total, arrive):
    blocks, rows, width = parts.shape[1:]
    wide = out.shape[3]
    copies = []
    for j in range(blocks):
        at = pl.ds(j * width, width)
        copies.append(pltpu.make_async_copy(parts.at[:, j], pair.at[:, j], arrive.at[0, j]))
        copies.append(pltpu.make_async_copy(basis.at[at], held.at[at], arrive.at[1, j]))
    copies.append(pltpu.make_async_copy(moment, flat, arrive.at[2, 0]))
    for copy in copies:
        copy.start()
    for j in range(blocks):
        copies[2 * j].wait()
        grad = (pair[0, j].astype(f32) + pair[1, j].astype(f32)).astype(bf16)
        copies[2 * j + 1].wait()
        part = jnp.dot(grad, held[j * width : (j + 1) * width], preferred_element_type=f32)
        if j == 0:
            total[...] = part
        elif j < blocks - 1:
            total[...] += part
        else:
            part = (total[...] + part).astype(bf16)
    copies[-1].wait()
    for i in range(out.shape[0]):
        out[i, 0] = part[:, i * wide : (i + 1) * wide]
        out[i, 1] = flat[:, i * wide : (i + 1) * wide].astype(bf16)


def half_rotate(parts, basis, moments, count):
    rows, order = moments.shape
    return pl.pallas_call(
        half_kernel,
        in_specs=[ANY] * 3,
        out_specs=VMEM,
        out_shape=jax.ShapeDtypeStruct((count, 2, rows, order // count), bf16),
        scratch_shapes=[
            pltpu.VMEM(parts.shape, bf16),
            pltpu.VMEM(basis.shape, bf16),
            pltpu.VMEM(moments.shape, f32),
            pltpu.VMEM(moments.shape, f32),
            pltpu.SemaphoreType.DMA((3, parts.shape[1])),
        ],
        compiler_params=limit(50),
        cost_estimate=pl.CostEstimate(
            flops=2 * rows * order * order, bytes_accessed=2 * order * order, transcendentals=0
        ),
        name="half_rotate",
    )(parts, basis, moments)


def stack_kernel(*refs):
    out = refs[-1]
    for i, ref in enumerate(refs[:-1]):
        out[i] = ref[...]


def stack(pieces):
    return pl.pallas_call(
        stack_kernel,
        in_specs=[VMEM] * len(pieces),
        out_specs=VMEM,
        out_shape=jax.ShapeDtypeStruct((len(pieces),) + pieces[0].shape, pieces[0].dtype),
        compiler_params=limit(8),
        cost_estimate=pl.CostEstimate(flops=0, bytes_accessed=1 << 25, transcendentals=0),
        name="stack",
    )(*pieces)


offsets = (0, -1, 1, -2, 2, -3, 3, 4)


def rotate_kernel(place, mine, *refs):
    sources, (out, flipped, scaled, held, arrive) = refs[:8], refs[8:]
    chip, core, first = place[0], place[1], place[2]
    starts = [lax.rem(first + i, 4) for i in (0, 3, 1, 2)]
    count, _, rows, width = out.shape
    chips, per = count // 2, count // 4
    copies = [
        [
            pltpu.make_async_copy(
                sources[i].at[pl.ds(2 * n, 2)], held.at[i, pl.ds(2 * n, 2)], arrive.at[n, i]
            )
            for i in range(8)
        ]
        for n in range(4)
    ]
    for some in copies:
        for copy in some:
            copy.start()
    for q in range(4):
        flipped[q] = mine[q * per : (q + 1) * per, 0].reshape(per * rows, width).T
    for n in range(8):
        if n % 2 == 0:
            for copy in copies[n // 2]:
                copy.wait()
        both = jnp.zeros((width, 2 * rows), f32)
        for q in range(4):
            rhs = jnp.concatenate(
                [held[4 * p + q, n].reshape(per * rows, rows) for p in range(2)], axis=1
            )
            both += jnp.dot(flipped[starts[q]], rhs, preferred_element_type=f32)
        for p in range(2):
            value = both[:, p * rows : (p + 1) * rows].T
            at = 2 * lax.rem(chip + offsets[n] + chips, chips) + (core if p == 0 else 1 - core)
            moment = mine[at, 1].astype(f32)
            out[at, 1] = value.astype(bf16)
            moment = ema_decay * moment + (1.0 - ema_decay) * value * value
            at = (2 * n + p) * rows
            scaled[at : at + rows] = (value / (moment + damping)).astype(bf16)
    for q in range(4):
        lhs = jnp.concatenate(
            [held[4 * p + q, n].reshape(per * rows, rows) for n in range(8) for p in range(2)],
            axis=1,
        )
        part = jnp.dot(lhs, scaled[...], preferred_element_type=f32)
        out[pl.ds(starts[q] * per, per), 0] = part.reshape(per, rows, width).astype(bf16)


def rotate(place, mine, sources):
    count, _, rows, width = mine.shape
    return pl.pallas_call(
        rotate_kernel,
        in_specs=[SMEM, VMEM] + [ANY] * 8,
        out_specs=VMEM,
        out_shape=jax.ShapeDtypeStruct(mine.shape, bf16),
        scratch_shapes=[
            pltpu.VMEM((4, width, count // 4 * rows), bf16),
            pltpu.VMEM((count * rows, width), bf16),
            pltpu.VMEM((8,) + sources[0].shape, bf16),
            pltpu.SemaphoreType.DMA((4, 8)),
        ],
        compiler_params=limit(24),
        cost_estimate=pl.CostEstimate(flops=1 << 32, bytes_accessed=1 << 25, transcendentals=0),
        name="rotate",
    )(place, mine, *sources)


def flip_kernel(source, out):
    step = 256
    for i in range(0, source.shape[0], step):
        for j in range(0, source.shape[1], step):
            out[j : j + step, i : i + step] = source[i : i + step, j : j + step].T


def flip(basis):
    return pl.pallas_call(
        flip_kernel,
        in_specs=[VMEM],
        out_specs=VMEM,
        out_shape=jax.ShapeDtypeStruct(basis.shape, basis.dtype),
        compiler_params=limit(8),
        cost_estimate=pl.CostEstimate(flops=0, bytes_accessed=4 * basis.size, transcendentals=0),
        name="flip",
    )(basis)


def update_kernel(back, basis, moment, update, moment_next, turned, fresh, leave):
    count, _, _, width = back.shape
    for i in range(count):
        at = slice(i * width, (i + 1) * width)
        turned[:, at] = back[i, 0]
        rotated = back[i, 1].astype(f32)
        fresh[i] = ema_decay * moment[:, at] + (1.0 - ema_decay) * rotated * rotated
        pltpu.make_async_copy(fresh.at[i], moment_next.at[:, i, 0], leave.at[i]).start()
    step = 256
    for i in range(0, basis.shape[1], step):
        update[:, i : i + step] = jnp.dot(
            turned[...], basis[:, i : i + step], preferred_element_type=f32
        ).astype(bf16)
    for i in range(count):
        pltpu.make_async_copy(fresh.at[i], moment_next.at[:, i, 0], leave.at[i]).wait()


def finish(back, basis, moments):
    rows, order = moments.shape
    count = back.shape[0]
    return pl.pallas_call(
        update_kernel,
        in_specs=[VMEM] * 3,
        out_specs=[VMEM, ANY],
        out_shape=[
            jax.ShapeDtypeStruct((rows, order), bf16),
            jax.ShapeDtypeStruct((rows, count, 1, order // count), f32),
        ],
        scratch_shapes=[
            pltpu.VMEM((rows, order), bf16),
            pltpu.VMEM((count, rows, order // count), f32),
            pltpu.SemaphoreType.DMA((count,)),
        ],
        compiler_params=limit(16),
        name="finish",
    )(back, basis, moments)


def shards(grad_parts, out_basis, in_basis, moments):
    rows, blocks, width = grad_parts.shape[2:]
    order = in_basis.shape[1]
    row, col = lax.axis_index("row"), lax.axis_index("col")
    count = lax.axis_size("row")
    chips = count // 2
    up = [(i, (i + 2) % count) for i in range(count)]
    down = [(b, a) for a, b in up]
    swap = [(i, i ^ 1) for i in range(count)]
    y_next = [(4 * h + y, 4 * h + (y + 1) % 4) for h in range(2) for y in range(4)]
    y_last = [(b, a) for a, b in y_next]
    x_swap = [(i, (i + 4) % 8) for i in range(8)]
    quarter = (col + 2 * (col >> 2)) & 3
    place = jnp.stack([row >> 1, row & 1, quarter]).astype(jnp.int32)

    own = lax.dynamic_slice_in_dim(out_basis[0], quarter * (order // 4), order // 4, 0)
    own = own.reshape(chips // 4, 2, rows, rows)
    a, b = lax.ppermute(own, "row", up), lax.ppermute(own, "row", down)

    sent = grad_parts[0].transpose(0, 2, 1, 3).reshape(-1, rows, width)
    parts = lax.all_to_all(sent, ("dp", "col"), split_axis=0, concat_axis=0, tiled=True)
    parts = parts.reshape(2, blocks, rows, width)

    near = [own, a, b]
    flat = moments.reshape(rows, order)
    a, b, flat = lax.optimization_barrier((a, b, flat))
    for _ in range(2):
        a, b = lax.ppermute(a, "row", up), lax.ppermute(b, "row", down)
        near += [a, b]
    near.append(lax.ppermute(near[3], "row", [(i, (i + 4) % count) for i in range(count)]))
    half = half_rotate(parts, in_basis[0], flat, count)
    first, near = lax.optimization_barrier((half, near))
    held = stack(near)
    quarters = [held]
    for pairs in (y_next, y_last, x_swap):
        quarters.append(lax.ppermute(held, "col", pairs))
    quarters += [lax.ppermute(x, "row", swap) for x in quarters]
    half = lax.all_to_all(half, "row", split_axis=0, concat_axis=0, tiled=True)
    half, flipped = lax.optimization_barrier((half, flip(lax.optimization_barrier((in_basis[0], held))[0])))
    back = rotate(place, half, quarters)
    back = lax.all_to_all(back, "row", split_axis=0, concat_axis=0, tiled=True)
    update, new_moments = finish(back, flipped, flat)
    return new_moments.reshape(1, rows, 1, order), update.reshape(1, rows, 1, order)


def solution(mesh):
    placed = (
        P("dp", None, "row", None, "col"),
        P("dp", None, "row"),
        P("col", None, None),
        P("dp", "row", "col", None),
    )
    return jax.shard_map(
        shards,
        mesh=mesh,
        in_specs=placed,
        out_specs=(P("dp", "row", "col", None), P("dp", "row", "col", None)),
        check_vma=False,
    )
```

```python
import jax
import jax.numpy as jnp
from jax import lax
from jax.experimental import pallas as pl
from jax.experimental.pallas import tpu as pltpu
from jax.sharding import PartitionSpec as P

ema_decay = 0.9
damping = 0.1
f32, bf16 = jnp.float32, jnp.bfloat16
VMEM = pl.BlockSpec(memory_space=pltpu.VMEM)
SMEM = pl.BlockSpec(memory_space=pltpu.SMEM)
ANY = pl.BlockSpec(memory_space=pl.ANY)


def limit(mib):
    return pltpu.CompilerParams(vmem_limit_bytes=mib * 1024 * 1024)


def half_kernel(parts, basis, moment, out, pair, held, flat, total, arrive):
    blocks, rows, width = parts.shape[1:]
    wide = out.shape[3]
    copies = []
    for j in range(blocks):
        at = pl.ds(j * width, width)
        copies.append(pltpu.make_async_copy(parts.at[:, j], pair.at[:, j], arrive.at[0, j]))
        copies.append(pltpu.make_async_copy(basis.at[at], held.at[at], arrive.at[1, j]))
    copies.append(pltpu.make_async_copy(moment, flat, arrive.at[2, 0]))
    for copy in copies:
        copy.start()
    for j in range(blocks):
        copies[2 * j].wait()
        grad = (pair[0, j].astype(f32) + pair[1, j].astype(f32)).astype(bf16)
        copies[2 * j + 1].wait()
        part = jnp.dot(grad, held[j * width : (j + 1) * width], preferred_element_type=f32)
        if j == 0:
            total[...] = part
        elif j < blocks - 1:
            total[...] += part
        else:
            part = (total[...] + part).astype(bf16)
    copies[-1].wait()
    for i in range(out.shape[0]):
        out[i, 0] = part[:, i * wide : (i + 1) * wide]
        out[i, 1] = flat[:, i * wide : (i + 1) * wide].astype(bf16)


def half_rotate(parts, basis, moments, count):
    rows, order = moments.shape
    return pl.pallas_call(
        half_kernel,
        in_specs=[ANY] * 3,
        out_specs=VMEM,
        out_shape=jax.ShapeDtypeStruct((count, 2, rows, order // count), bf16),
        scratch_shapes=[
            pltpu.VMEM(parts.shape, bf16),
            pltpu.VMEM(basis.shape, bf16),
            pltpu.VMEM(moments.shape, f32),
            pltpu.VMEM(moments.shape, f32),
            pltpu.SemaphoreType.DMA((3, parts.shape[1])),
        ],
        compiler_params=limit(50),
        cost_estimate=pl.CostEstimate(
            flops=2 * rows * order * order, bytes_accessed=2 * order * order, transcendentals=0
        ),
        name="half_rotate",
    )(parts, basis, moments)


def stack_kernel(*refs):
    out = refs[-1]
    for i, ref in enumerate(refs[:-1]):
        out[i] = ref[...]


def stack(pieces):
    return pl.pallas_call(
        stack_kernel,
        in_specs=[VMEM] * len(pieces),
        out_specs=VMEM,
        out_shape=jax.ShapeDtypeStruct((len(pieces),) + pieces[0].shape, pieces[0].dtype),
        compiler_params=limit(8),
        cost_estimate=pl.CostEstimate(flops=0, bytes_accessed=1 << 25, transcendentals=0),
        name="stack",
    )(*pieces)


offsets = (0, -1, 1, -2, 2, -3, 3, 4)


def rotate_kernel(place, mine, *refs):
    sources, (out, flipped, scaled, held, arrive) = refs[:8], refs[8:]
    chip, core, first = place[0], place[1], place[2]
    starts = [lax.rem(first + i, 4) for i in (0, 3, 1, 2)]
    count, _, rows, width = out.shape
    chips, per = count // 2, count // 4
    copies = [
        [
            pltpu.make_async_copy(
                sources[i].at[pl.ds(2 * n, 2)], held.at[i, pl.ds(2 * n, 2)], arrive.at[n, i]
            )
            for i in range(8)
        ]
        for n in range(4)
    ]
    for some in copies:
        for copy in some:
            copy.start()
    for q in range(4):
        flipped[q] = mine[q * per : (q + 1) * per, 0].reshape(per * rows, width).T
    for n in range(8):
        if n % 2 == 0:
            for copy in copies[n // 2]:
                copy.wait()
        both = jnp.zeros((width, 2 * rows), f32)
        for q in range(4):
            rhs = jnp.concatenate(
                [held[4 * p + q, n].reshape(per * rows, rows) for p in range(2)], axis=1
            )
            both += jnp.dot(flipped[starts[q]], rhs, preferred_element_type=f32)
        for p in range(2):
            value = both[:, p * rows : (p + 1) * rows].T
            at = 2 * lax.rem(chip + offsets[n] + chips, chips) + (core if p == 0 else 1 - core)
            moment = mine[at, 1].astype(f32)
            out[at, 1] = value.astype(bf16)
            moment = ema_decay * moment + (1.0 - ema_decay) * value * value
            at = (2 * n + p) * rows
            scaled[at : at + rows] = (value / (moment + damping)).astype(bf16)
    for q in range(4):
        lhs = jnp.concatenate(
            [held[4 * p + q, n].reshape(per * rows, rows) for n in range(8) for p in range(2)],
            axis=1,
        )
        part = jnp.dot(lhs, scaled[...], preferred_element_type=f32)
        out[pl.ds(starts[q] * per, per), 0] = part.reshape(per, rows, width).astype(bf16)


def rotate(place, mine, sources):
    count, _, rows, width = mine.shape
    return pl.pallas_call(
        rotate_kernel,
        in_specs=[SMEM, VMEM] + [ANY] * 8,
        out_specs=VMEM,
        out_shape=jax.ShapeDtypeStruct(mine.shape, bf16),
        scratch_shapes=[
            pltpu.VMEM((4, width, count // 4 * rows), bf16),
            pltpu.VMEM((count * rows, width), bf16),
            pltpu.VMEM((8,) + sources[0].shape, bf16),
            pltpu.SemaphoreType.DMA((4, 8)),
        ],
        compiler_params=limit(24),
        cost_estimate=pl.CostEstimate(flops=1 << 32, bytes_accessed=1 << 25, transcendentals=0),
        name="rotate",
    )(place, mine, *sources)


def flip_kernel(source, out, held, turned, arrive, leave):
    step = 256
    spans = [pl.ds(i, step) for i in range(0, source.shape[0], step)]
    ins = [
        pltpu.make_async_copy(source.at[at], held.at[at], arrive.at[i]) for i, at in enumerate(spans)
    ]
    outs = [
        pltpu.make_async_copy(turned.at[:, at], out.at[:, at], leave.at[i])
        for i, at in enumerate(spans)
    ]
    for copy in ins:
        copy.start()
    for i in range(len(spans)):
        ins[i].wait()
        rows = slice(i * step, (i + 1) * step)
        for j in range(0, source.shape[1], step):
            turned[j : j + step, rows] = held[rows, j : j + step].T
        outs[i].start()
    for copy in outs:
        copy.wait()


def flip(basis):
    return pl.pallas_call(
        flip_kernel,
        in_specs=[ANY],
        out_specs=ANY,
        out_shape=jax.ShapeDtypeStruct(basis.shape, basis.dtype),
        scratch_shapes=[
            pltpu.VMEM(basis.shape, basis.dtype),
            pltpu.VMEM(basis.shape, basis.dtype),
            pltpu.SemaphoreType.DMA((8,)),
            pltpu.SemaphoreType.DMA((8,)),
        ],
        compiler_params=limit(50),
        cost_estimate=pl.CostEstimate(flops=0, bytes_accessed=4 * basis.size, transcendentals=0),
        name="flip",
    )(basis)


def update_kernel(back, basis, moment, update, moment_next, turned, fresh, leave):
    count, _, _, width = back.shape
    for i in range(count):
        at = slice(i * width, (i + 1) * width)
        turned[:, at] = back[i, 0]
        rotated = back[i, 1].astype(f32)
        fresh[i] = ema_decay * moment[:, at] + (1.0 - ema_decay) * rotated * rotated
        pltpu.make_async_copy(fresh.at[i], moment_next.at[:, i, 0], leave.at[i]).start()
    step = 256
    for i in range(0, basis.shape[1], step):
        update[:, i : i + step] = jnp.dot(
            turned[...], basis[:, i : i + step], preferred_element_type=f32
        ).astype(bf16)
    for i in range(count):
        pltpu.make_async_copy(fresh.at[i], moment_next.at[:, i, 0], leave.at[i]).wait()


def finish(back, basis, moments):
    rows, order = moments.shape
    count = back.shape[0]
    return pl.pallas_call(
        update_kernel,
        in_specs=[VMEM] * 3,
        out_specs=[VMEM, ANY],
        out_shape=[
            jax.ShapeDtypeStruct((rows, order), bf16),
            jax.ShapeDtypeStruct((rows, count, 1, order // count), f32),
        ],
        scratch_shapes=[
            pltpu.VMEM((rows, order), bf16),
            pltpu.VMEM((count, rows, order // count), f32),
            pltpu.SemaphoreType.DMA((count,)),
        ],
        compiler_params=limit(16),
        name="finish",
    )(back, basis, moments)


def shards(grad_parts, out_basis, in_basis, moments):
    rows, blocks, width = grad_parts.shape[2:]
    order = in_basis.shape[1]
    row, col = lax.axis_index("row"), lax.axis_index("col")
    count = lax.axis_size("row")
    chips = count // 2
    up = [(i, (i + 2) % count) for i in range(count)]
    down = [(b, a) for a, b in up]
    swap = [(i, i ^ 1) for i in range(count)]
    y_next = [(4 * h + y, 4 * h + (y + 1) % 4) for h in range(2) for y in range(4)]
    y_last = [(b, a) for a, b in y_next]
    x_swap = [(i, (i + 4) % 8) for i in range(8)]
    quarter = (col + 2 * (col >> 2)) & 3
    place = jnp.stack([row >> 1, row & 1, quarter]).astype(jnp.int32)

    own = lax.dynamic_slice_in_dim(out_basis[0], quarter * (order // 4), order // 4, 0)
    own = own.reshape(chips // 4, 2, rows, rows)
    a, b = lax.ppermute(own, "row", up), lax.ppermute(own, "row", down)

    sent = grad_parts[0].transpose(0, 2, 1, 3).reshape(-1, rows, width)
    parts = lax.all_to_all(sent, ("dp", "col"), split_axis=0, concat_axis=0, tiled=True)
    parts = parts.reshape(2, blocks, rows, width)

    near = [own, a, b]
    flat = moments.reshape(rows, order)
    a, b, flat = lax.optimization_barrier((a, b, flat))
    for _ in range(2):
        a, b = lax.ppermute(a, "row", up), lax.ppermute(b, "row", down)
        near += [a, b]
    near.append(lax.ppermute(near[3], "row", [(i, (i + 4) % count) for i in range(count)]))
    half = half_rotate(parts, in_basis[0], flat, count)
    first, near = lax.optimization_barrier((half, near))
    held = stack(near)
    quarters = [held]
    for pairs in (y_next, y_last, x_swap):
        quarters.append(lax.ppermute(held, "col", pairs))
    quarters += [lax.ppermute(x, "row", swap) for x in quarters]
    half = lax.all_to_all(half, "row", split_axis=0, concat_axis=0, tiled=True)
    half, flipped = lax.optimization_barrier((half, flip(lax.optimization_barrier((in_basis[0], held))[0])))
    back = rotate(place, half, quarters)
    back = lax.all_to_all(back, "row", split_axis=0, concat_axis=0, tiled=True)
    update, new_moments = finish(back, flipped, flat)
    return new_moments.reshape(1, rows, 1, order), update.reshape(1, rows, 1, order)


def solution(mesh):
    placed = (
        P("dp", None, "row", None, "col"),
        P("dp", None, "row"),
        P("col", None, None),
        P("dp", "row", "col", None),
    )
    return jax.shard_map(
        shards,
        mesh=mesh,
        in_specs=placed,
        out_specs=(P("dp", "row", "col", None), P("dp", "row", "col", None)),
        check_vma=False,
    )
```
